32 devices in a mesh: groups: 2 (over x), col: 8 (over z, y), row: 2 (over core).
Axes of the slice: x: 2, y: 2, z: 4, core: 2. Of those that a mesh axis runs over, the one named last changes fastest.
Arguments:
- points: bfloat16 [64, 3072], P(None, ('groups', 'col', 'row')), parts along dimension 1, may hold values from -6 to 6
- sketch: float32 [3072, 256], P(('groups', 'col', 'row')), parts along dimension 0, may hold values from -6 to 6
Outputs:
- basis: float32 [3072, 256], P(('groups', 'col', 'row')), parts along dimension 0
- factor: float32 [512, 256], P('groups'), parts along dimension 0
The draws below stay inside these ranges and needn't reach their ends.
There are 2 independent parts, one for each index of `groups`. The reference program is written for one: setup_inputs(seed, part) draws one part's arguments, and reference() takes and returns one part's arrays. A program takes and returns all parts, laid end to end along the dimension named above; each array names one. Nothing has to cross between parts.
All inputs are finite; a program needn't handle non-finite values.
Results may differ from the reference program's by a relative error of at most 0.0003.
Values may be sent and summed in bfloat16 or wider, within the bound.
A program may use at most 64 MiB of HBM per device.

```python
import math
import jax
import jax.numpy as jnp
from jax import lax

F = 64
K = 256
PASSES = 2
N = 1536


def level_of(rng, dims, shards, low, high):
    factor_of = 1.0
    for dim, parts in shards:
        steps = jax.random.uniform(jax.random.fold_in(jax.random.fold_in(rng, 6), dim), (parts,), jnp.float32, low / len(shards), high / len(shards))
        factor_of = factor_of * jnp.repeat(jnp.exp(steps), dims[dim] // parts).reshape((-1,) + (1,) * (len(dims) - 1 - dim))
    return factor_of


def scatter_about(rng, extent, deviation, reach, cuts=(), dtype=jnp.bfloat16):
    entries = deviation * jax.random.normal(rng, extent, jnp.float32)
    if cuts:
        entries = entries * level_of(rng, extent, cuts, -0.22, 0.18)
    return jnp.clip(entries, -reach, reach).astype(dtype)


def setup_inputs(seed: int = 0, part: int = 0) -> dict:
    seeds = jax.random.split(jax.random.key(seed), 3)
    part_keys = jax.random.split(jax.random.fold_in(seeds[2], part), 3)
    return {
        "points": scatter_about(part_keys[0], (F, N), 1.0, 6.0, ((1, 16),)),
        "sketch": scatter_about(part_keys[1], (N, K), 1.0, 6.0, ((0, 16),), jnp.float32),
    }


def kernel_rows(block_t, all_t, all_sq, gamma):
    block_f = block_t.astype(jnp.float32)
    block_sq = jnp.sum(block_f * block_f, axis=0)
    cross = lax.dot_general(block_t.astype(jnp.float32), all_t.astype(jnp.float32), (((0,), (0,)), ((), ())), preferred_element_type=jnp.float32)
    return jnp.exp(-gamma * (block_sq[:, None] + all_sq[None, :] - 2.0 * cross))

def orthonormal(ymat, block_count):
    gram = jnp.dot(ymat.T, ymat, precision=lax.Precision.HIGHEST) / block_count
    lower = jnp.linalg.cholesky(gram)
    qmat = jax.scipy.linalg.solve_triangular(lower, ymat.T, lower=True).T
    return (qmat, lower.T)

def reference(points, sketch):
    feats, block_count = points.shape
    gamma = ((block_count / 32.0) ** (2.0 / feats) - 1.0) / 4.0
    all_f = points.astype(jnp.float32)
    all_sq = jnp.sum(all_f * all_f, axis=0)
    width = math.gcd(block_count, 1024)
    block_list = points.reshape(feats, block_count // width, width).transpose(1, 0, 2)

    def apply_operator(vector_matrix):

        def single_entry(block_t):
            kernel_tile = kernel_rows(block_t, points, all_sq, gamma)
            return jnp.dot(kernel_tile.astype(jnp.float32), vector_matrix.astype(jnp.float32), precision=lax.Precision.HIGHEST, preferred_element_type=jnp.float32)
        return lax.map(single_entry, block_list).reshape(block_count, vector_matrix.shape[1])
    ymat = apply_operator(sketch)
    for step in range(PASSES):
        qmat, upper = orthonormal(ymat, block_count)
        ymat = apply_operator(qmat)
    basis, factor = orthonormal(ymat, block_count)
    return (basis, factor)
```

```python
import functools

import jax
import jax.numpy as jnp
from jax import lax
from jax.experimental import pallas as pl
from jax.experimental.pallas import tpu as pltpu
from jax.sharding import PartitionSpec as P

PASSES = 2
HIGHEST = lax.Precision.HIGHEST
MAX_POINTS = 2048
ROWS = 256
HALF = 128


def dot(a, b, dims, precision=None):
    return lax.dot_general(
        a, b, (dims, ((), ())), precision=precision, preferred_element_type=jnp.float32
    )


def split(x):
    high = x.astype(jnp.bfloat16)
    low = (x - high.astype(jnp.float32)).astype(jnp.bfloat16)
    return high, low


def factor_block(block):
    row = lax.broadcasted_iota(jnp.int32, (HALF, HALF), 0)
    lane = lax.broadcasted_iota(jnp.int32, (HALF, HALF), 1)
    sub = lax.broadcasted_iota(jnp.int32, (8, HALF), 0)
    a = block
    i = jnp.where(row == lane, 1.0, 0.0).astype(jnp.float32)
    done_a, done_i = [], []
    for k in range(0, HALF, 8):
        cols = [jnp.broadcast_to(a[:, k + j : k + j + 1], a.shape) for j in range(8)]
        head_a, head_i = a[:8], i[:8]
        mults, rows_a, rows_i = [], [], []
        for j in range(8):
            r = lax.rsqrt(cols[j][j : j + 1])
            m = cols[j] * r
            for n in range(j + 1, 8):
                cols[n] = cols[n] - m * (cols[n][j : j + 1] * r)
            row_a, row_i = head_a[j : j + 1] * r, head_i[j : j + 1] * r
            below = jnp.where(sub > j, m[:8], 0.0)
            head_a = jnp.where(sub == j, row_a, head_a - below * row_a)
            head_i = jnp.where(sub == j, row_i, head_i - below * row_i)
            mults.append(m)
            rows_a.append(row_a)
            rows_i.append(row_i)
        done_a.append(head_a)
        done_i.append(head_i)
        if k + 8 < HALF:
            a, i = a[8:], i[8:]
            for j in range(8):
                a = a - mults[j][8:] * rows_a[j]
                i = i - mults[j][8:] * rows_i[j]
    upper = jnp.where(row <= lane, jnp.concatenate(done_a, axis=0), 0.0)
    return upper, jnp.concatenate(done_i, axis=0)


def part_kernel(gamma, pts, sketch, basis, factor, high, low, v, vh, vl, y, inv):
    feats, count = pts.shape
    own = basis.shape[0]
    me = lax.axis_index("col") * lax.axis_size("row") + lax.axis_index("row")
    all_f = pts[...].astype(jnp.float32)
    all_sq = jnp.sum(all_f * all_f, axis=0, keepdims=True)
    ones = jnp.ones((feats, HALF), jnp.float32)
    for at in range(0, count, ROWS):
        rows = pts[:, at : at + ROWS]
        rows_f = rows.astype(jnp.float32)
        rows_sq = dot(rows_f * rows_f, ones, ((0,), (0,)), HIGHEST)[:, :1]
        cross = dot(rows, pts[...], ((0,), (0,)))
        h, l = split(jnp.exp(-gamma * (rows_sq + all_sq - 2.0 * cross)))
        high[at : at + ROWS] = h
        low[at : at + ROWS] = l
    v[...] = sketch[...]

    def one_pass(step, carry):
        h, l = split(v[...])
        vh[...] = h
        vl[...] = l

        def apply_rows(b, c):
            at = pl.ds(pl.multiple_of(b * ROWS, ROWS), ROWS)
            kh, kl = high[at, :], low[at, :]
            d = ((1,), (0,))
            y[at, :] = dot(kh, vh[...], d) + (dot(kh, vl[...], d) + dot(kl, vh[...], d))
            return c

        lax.fori_loop(0, count // ROWS, apply_rows, 0)
        ym = y[...]
        gram = dot(ym, ym, ((0,), (0,)), HIGHEST) / count
        u11, i11 = factor_block(gram[:HALF, :HALF])
        u12 = dot(i11, gram[:HALF, HALF:], ((1,), (0,)), HIGHEST)
        rest = gram[HALF:, HALF:] - dot(u12, u12, ((0,), (0,)), HIGHEST)
        u22, i22 = factor_block(rest)
        i21 = -dot(i22, dot(u12, i11, ((0,), (0,)), HIGHEST), ((1,), (0,)), HIGHEST)
        factor[:HALF, :HALF] = u11
        factor[:HALF, HALF:] = u12
        factor[HALF:, :HALF] = jnp.zeros_like(u11)
        factor[HALF:, HALF:] = u22
        inv[:HALF, :HALF] = i11
        inv[:HALF, HALF:] = jnp.zeros_like(i11)
        inv[HALF:, :HALF] = i21
        inv[HALF:, HALF:] = i22
        v[...] = dot(ym, inv[...], ((1,), (1,)), HIGHEST)
        return carry

    lax.fori_loop(0, PASSES + 1, one_pass, 0)
    basis[...] = v[pl.ds(pl.multiple_of(me * own, 8), own), :]


def whole_part(points, sketch):
    feats, own = points.shape
    rank = sketch.shape[1]
    count = own * lax.axis_size("col") * lax.axis_size("row")
    gamma = ((count / 32.0) ** (2.0 / feats) - 1.0) / 4.0
    pts = lax.all_gather(points, ("col", "row"), axis=1, tiled=True)
    full = lax.all_gather(sketch, ("col", "row"), axis=0, tiled=True)
    return pl.pallas_call(
        functools.partial(part_kernel, gamma),
        out_shape=(
            jax.ShapeDtypeStruct((own, rank), jnp.float32),
            jax.ShapeDtypeStruct((rank, rank), jnp.float32),
        ),
        in_specs=[pl.BlockSpec(memory_space=pltpu.VMEM)] * 2,
        out_specs=[pl.BlockSpec(memory_space=pltpu.VMEM)] * 2,
        scratch_shapes=[
            pltpu.VMEM((count, count), jnp.bfloat16),
            pltpu.VMEM((count, count), jnp.bfloat16),
            pltpu.VMEM((count, rank), jnp.float32),
            pltpu.VMEM((count, rank), jnp.bfloat16),
            pltpu.VMEM((count, rank), jnp.bfloat16),
            pltpu.VMEM((count, rank), jnp.float32),
            pltpu.VMEM((rank, rank), jnp.float32),
        ],
        compiler_params=pltpu.CompilerParams(vmem_limit_bytes=50 * 1024 * 1024),
    )(pts, full)


def kernel_rows(block_t, cols_t, gamma):
    block_f = block_t.astype(jnp.float32)
    cols_f = cols_t.astype(jnp.float32)
    block_sq = jnp.sum(block_f * block_f, axis=0)
    cols_sq = jnp.sum(cols_f * cols_f, axis=0)
    cross = lax.dot_general(
        block_t, cols_t, (((0,), (0,)), ((), ())), preferred_element_type=jnp.float32
    )
    return jnp.exp(-gamma * (block_sq[:, None] + cols_sq[None, :] - 2.0 * cross))


def orthonormal(ymat, block_count):
    local_gram = jnp.dot(ymat.T, ymat, precision=lax.Precision.HIGHEST)
    gram = lax.psum(local_gram, ("col", "row")) / block_count
    lower = jnp.linalg.cholesky(gram)
    qmat = jax.scipy.linalg.solve_triangular(lower, ymat.T, lower=True).T
    return (qmat, lower.T)


def split_part(points, sketch):
    feats, own = points.shape
    block_count = own * lax.axis_size("col") * lax.axis_size("row")
    gamma = ((block_count / 32.0) ** (2.0 / feats) - 1.0) / 4.0
    row_pts = lax.all_gather(points, "row", axis=1, tiled=True)
    col_pts = lax.all_gather(points, "col", axis=1, tiled=True)

    def tile_at():
        return kernel_rows(row_pts, col_pts, gamma)

    def accumulate_fragment(piece):
        kernel_tile = tile_at()
        return jnp.dot(
            kernel_tile, piece, precision=lax.Precision.HIGHEST, preferred_element_type=jnp.float32
        )

    def apply_operator(vector_matrix):
        running_sum = accumulate_fragment(lax.all_gather(vector_matrix, "col", axis=0, tiled=True))
        return lax.psum_scatter(running_sum, "row", scatter_dimension=0, tiled=True)

    ymat = apply_operator(sketch)
    for step in range(PASSES):
        qmat, upper = orthonormal(ymat, block_count)
        ymat = apply_operator(qmat)
    basis, factor = orthonormal(ymat, block_count)
    return (basis, factor)


def local(points, sketch):
    count = points.shape[1] * lax.axis_size("col") * lax.axis_size("row")
    small = count <= MAX_POINTS and count % ROWS == 0
    if small and sketch.shape[1] == 2 * HALF and points.shape[1] % 8 == 0:
        return whole_part(points, sketch)
    return split_part(points, sketch)


def solution(mesh):
    in_specs = (P(None, ("groups", "col", "row")), P(("groups", "col", "row"), None))
    out_specs = (P(("groups", "col", "row"), None), P("groups", None))
    return jax.shard_map(local, mesh=mesh, in_specs=in_specs, out_specs=out_specs, check_vma=False)
```

```python
import functools

import jax
import jax.numpy as jnp
from jax import lax
from jax.experimental import pallas as pl
from jax.experimental.pallas import tpu as pltpu
from jax.sharding import PartitionSpec as P

PASSES = 2
HIGHEST = lax.Precision.HIGHEST
MAX_POINTS = 2048
ROWS = 256
HALF = 128
MESH = pl.DeviceIdType.MESH


def dot(a, b, dims, precision=None):
    return lax.dot_general(
        a, b, (dims, ((), ())), precision=precision, preferred_element_type=jnp.float32
    )


def split(x):
    high = x.astype(jnp.bfloat16)
    low = (x - high.astype(jnp.float32)).astype(jnp.bfloat16)
    return high, low


def factor_block(block):
    row = lax.broadcasted_iota(jnp.int32, (HALF, HALF), 0)
    lane = lax.broadcasted_iota(jnp.int32, (HALF, HALF), 1)
    sub = lax.broadcasted_iota(jnp.int32, (8, HALF), 0)
    a = block
    i = jnp.where(row == lane, 1.0, 0.0).astype(jnp.float32)
    done_a, done_i = [], []
    for k in range(0, HALF, 8):
        cols = [jnp.broadcast_to(a[:, k + j : k + j + 1], a.shape) for j in range(8)]
        head_a, head_i = a[:8], i[:8]
        mults, rows_a, rows_i = [], [], []
        for j in range(8):
            r = lax.rsqrt(cols[j][j : j + 1])
            m = cols[j] * r
            for n in range(j + 1, 8):
                cols[n] = cols[n] - m * (cols[n][j : j + 1] * r)
            row_a, row_i = head_a[j : j + 1] * r, head_i[j : j + 1] * r
            below = jnp.where(sub > j, m[:8], 0.0)
            head_a = jnp.where(sub == j, row_a, head_a - below * row_a)
            head_i = jnp.where(sub == j, row_i, head_i - below * row_i)
            mults.append(m)
            rows_a.append(row_a)
            rows_i.append(row_i)
        done_a.append(head_a)
        done_i.append(head_i)
        if k + 8 < HALF:
            a, i = a[8:], i[8:]
            for j in range(8):
                a = a - mults[j][8:] * rows_a[j]
                i = i - mults[j][8:] * rows_i[j]
    upper = jnp.where(row <= lane, jnp.concatenate(done_a, axis=0), 0.0)
    return upper, jnp.concatenate(done_i, axis=0)


def gather_kernel(own_pts, own_sketch, pts, sketch, *sems):
    own = own_sketch.shape[0]
    group = lax.axis_index("groups")
    col, core = lax.axis_index("col"), lax.axis_index("row")
    depth = lax.axis_size("col") // 2
    z, y = col // 2, lax.rem(col, 2)

    def device(z_of, y_of, core_of):
        return (group, z_of * 2 + y_of, core_of)

    def rows(z_of, y_of, core_of):
        slot = (core_of * 2 + y_of) * depth + z_of
        return pl.ds(pl.multiple_of(slot * own, 16), own)

    along_z = [device(lax.rem(z + d, depth), y, core) for d in range(1, depth)]
    y_peer, core_peer = device(z, 1 - y, core), device(z, y, 1 - core)
    barrier = pltpu.get_barrier_semaphore()
    for peer in along_z + [y_peer, core_peer]:
        pl.semaphore_signal(barrier, inc=1, device_id=peer, device_id_type=MESH)
    mine = rows(z, y, core)
    pts[mine, :] = own_pts[...]
    sketch[mine, :] = own_sketch[...]
    pl.semaphore_wait(barrier, depth + 1)

    def send(full, at, peer, number, send_sem, recv_sem):
        copy = pltpu.make_async_remote_copy(
            src_ref=full.at[at, :],
            dst_ref=full.at[at, :],
            send_sem=send_sem.at[number],
            recv_sem=recv_sem.at[number],
            device_id=peer,
            device_id_type=MESH,
        )
        copy.start()
        return copy

    arrays = [(pts, sems[0], sems[1]), (sketch, sems[2], sems[3])]
    z_copies, y_copies, c_copies = [[], []], [[], []], [[], []]
    y_base, c_base = depth - 1, 2 * depth - 1
    for n, (full, ss, rs) in enumerate(arrays):
        for d in range(1, depth):
            z_copies[n].append(send(full, mine, along_z[d - 1], d - 1, ss, rs))
        y_copies[n].append(send(full, mine, y_peer, y_base, ss, rs))
        c_copies[n].append(send(full, mine, core_peer, c_base, ss, rs))
    for n, (full, ss, rs) in enumerate(arrays):
        for d in range(1, depth):
            at = rows(lax.rem(z - d + depth, depth), y, core)
            z_copies[n][d - 1].wait_recv()
            y_copies[n].append(send(full, at, y_peer, y_base + d, ss, rs))
            c_copies[n].append(send(full, at, core_peer, c_base + d, ss, rs))
        for d in range(depth):
            at = rows(lax.rem(z - d + depth, depth), 1 - y, core)
            y_copies[n][d].wait_recv()
            c_copies[n].append(send(full, at, core_peer, c_base + depth + d, ss, rs))
    for n in range(2):
        for copy in c_copies[n]:
            copy.wait_recv()
        for copy in z_copies[n] + y_copies[n] + c_copies[n]:
            copy.wait_send()


def part_kernel(gamma, pts, sketch, basis, factor, high, low, v, vh, vl, y, inv):
    count, feats = pts.shape
    own = basis.shape[0]
    col, core = lax.axis_index("col"), lax.axis_index("row")
    me = (core * 2 + lax.rem(col, 2)) * (lax.axis_size("col") // 2) + col // 2
    all_f = pts[...].astype(jnp.float32)
    ones = jnp.ones((8, feats), jnp.float32)
    all_sq = dot(ones, all_f * all_f, ((1,), (1,)), HIGHEST)[:1]
    for at in range(0, count, ROWS):
        rows = pts[at : at + ROWS, :]
        rows_f = rows.astype(jnp.float32)
        rows_sq = jnp.sum(rows_f * rows_f, axis=1, keepdims=True)
        cross = dot(rows, pts[...], ((1,), (1,)))
        h, l = split(jnp.exp(-gamma * (rows_sq + all_sq - 2.0 * cross)))
        high[at : at + ROWS] = h
        low[at : at + ROWS] = l
    v[...] = sketch[...]

    def one_pass(step, carry):
        h, l = split(v[...])
        vh[...] = h
        vl[...] = l

        def apply_rows(b, c):
            at = pl.ds(pl.multiple_of(b * ROWS, ROWS), ROWS)
            kh, kl = high[at, :], low[at, :]
            d = ((1,), (0,))
            y[at, :] = dot(kh, vh[...], d) + (dot(kh, vl[...], d) + dot(kl, vh[...], d))
            return c

        lax.fori_loop(0, count // ROWS, apply_rows, 0)
        ym = y[...]
        gram = dot(ym, ym, ((0,), (0,)), HIGHEST) / count
        u11, i11 = factor_block(gram[:HALF, :HALF])
        u12 = dot(i11, gram[:HALF, HALF:], ((1,), (0,)), HIGHEST)
        rest = gram[HALF:, HALF:] - dot(u12, u12, ((0,), (0,)), HIGHEST)
        u22, i22 = factor_block(rest)
        i21 = -dot(i22, dot(u12, i11, ((0,), (0,)), HIGHEST), ((1,), (0,)), HIGHEST)
        factor[:HALF, :HALF] = u11
        factor[:HALF, HALF:] = u12
        factor[HALF:, :HALF] = jnp.zeros_like(u11)
        factor[HALF:, HALF:] = u22
        inv[:HALF, :HALF] = i11
        inv[:HALF, HALF:] = jnp.zeros_like(i11)
        inv[HALF:, :HALF] = i21
        inv[HALF:, HALF:] = i22
        v[...] = dot(ym, inv[...], ((1,), (1,)), HIGHEST)
        return carry

    lax.fori_loop(0, PASSES + 1, one_pass, 0)
    basis[...] = v[pl.ds(pl.multiple_of(me * own, 8), own), :]


def whole_part(points, sketch):
    feats, own = points.shape
    rank = sketch.shape[1]
    count = own * lax.axis_size("col") * lax.axis_size("row")
    gamma = ((count / 32.0) ** (2.0 / feats) - 1.0) / 4.0
    copies = 2 * (lax.axis_size("col") // 2) * 2 - 1
    pts, full = pl.pallas_call(
        gather_kernel,
        out_shape=(
            jax.ShapeDtypeStruct((count, feats), points.dtype),
            jax.ShapeDtypeStruct((count, rank), sketch.dtype),
        ),
        in_specs=[pl.BlockSpec(memory_space=pltpu.VMEM)] * 2,
        out_specs=[pl.BlockSpec(memory_space=pltpu.VMEM)] * 2,
        scratch_shapes=[pltpu.SemaphoreType.DMA((copies,))] * 4,
        compiler_params=pltpu.CompilerParams(
            collective_id=0, has_side_effects=True, vmem_limit_bytes=8 * 1024 * 1024
        ),
    )(points.T, sketch)
    return pl.pallas_call(
        functools.partial(part_kernel, gamma),
        out_shape=(
            jax.ShapeDtypeStruct((own, rank), jnp.float32),
            jax.ShapeDtypeStruct((rank, rank), jnp.float32),
        ),
        in_specs=[pl.BlockSpec(memory_space=pltpu.VMEM)] * 2,
        out_specs=[pl.BlockSpec(memory_space=pltpu.VMEM)] * 2,
        scratch_shapes=[
            pltpu.VMEM((count, count), jnp.bfloat16),
            pltpu.VMEM((count, count), jnp.bfloat16),
            pltpu.VMEM((count, rank), jnp.float32),
            pltpu.VMEM((count, rank), jnp.bfloat16),
            pltpu.VMEM((count, rank), jnp.bfloat16),
            pltpu.VMEM((count, rank), jnp.float32),
            pltpu.VMEM((rank, rank), jnp.float32),
        ],
        compiler_params=pltpu.CompilerParams(vmem_limit_bytes=50 * 1024 * 1024),
    )(pts, full)


def kernel_rows(block_t, cols_t, gamma):
    block_f = block_t.astype(jnp.float32)
    cols_f = cols_t.astype(jnp.float32)
    block_sq = jnp.sum(block_f * block_f, axis=0)
    cols_sq = jnp.sum(cols_f * cols_f, axis=0)
    cross = lax.dot_general(
        block_t, cols_t, (((0,), (0,)), ((), ())), preferred_element_type=jnp.float32
    )
    return jnp.exp(-gamma * (block_sq[:, None] + cols_sq[None, :] - 2.0 * cross))


def orthonormal(ymat, block_count):
    local_gram = jnp.dot(ymat.T, ymat, precision=lax.Precision.HIGHEST)
    gram = lax.psum(local_gram, ("col", "row")) / block_count
    lower = jnp.linalg.cholesky(gram)
    qmat = jax.scipy.linalg.solve_triangular(lower, ymat.T, lower=True).T
    return (qmat, lower.T)


def split_part(points, sketch):
    feats, own = points.shape
    block_count = own * lax.axis_size("col") * lax.axis_size("row")
    gamma = ((block_count / 32.0) ** (2.0 / feats) - 1.0) / 4.0
    row_pts = lax.all_gather(points, "row", axis=1, tiled=True)
    col_pts = lax.all_gather(points, "col", axis=1, tiled=True)

    def tile_at():
        return kernel_rows(row_pts, col_pts, gamma)

    def accumulate_fragment(piece):
        kernel_tile = tile_at()
        return jnp.dot(
            kernel_tile, piece, precision=lax.Precision.HIGHEST, preferred_element_type=jnp.float32
        )

    def apply_operator(vector_matrix):
        running_sum = accumulate_fragment(lax.all_gather(vector_matrix, "col", axis=0, tiled=True))
        return lax.psum_scatter(running_sum, "row", scatter_dimension=0, tiled=True)

    ymat = apply_operator(sketch)
    for step in range(PASSES):
        qmat, upper = orthonormal(ymat, block_count)
        ymat = apply_operator(qmat)
    basis, factor = orthonormal(ymat, block_count)
    return (basis, factor)


def local(points, sketch):
    count = points.shape[1] * lax.axis_size("col") * lax.axis_size("row")
    small = count <= MAX_POINTS and count % ROWS == 0
    pairs = lax.axis_size("col") % 2 == 0 and lax.axis_size("row") == 2
    if small and pairs and sketch.shape[1] == 2 * HALF and points.shape[1] % 16 == 0:
        return whole_part(points, sketch)
    return split_part(points, sketch)


def solution(mesh):
    in_specs = (P(None, ("groups", "col", "row")), P(("groups", "col", "row"), None))
    out_specs = (P(("groups", "col", "row"), None), P("groups", None))
    return jax.shard_map(local, mesh=mesh, in_specs=in_specs, out_specs=out_specs, check_vma=False)
```

```python
import functools

import jax
import jax.numpy as jnp
from jax import lax
from jax.experimental import pallas as pl
from jax.experimental.pallas import tpu as pltpu
from jax.sharding import PartitionSpec as P

PASSES = 2
HIGHEST = lax.Precision.HIGHEST
MAX_POINTS = 2048
ROWS = 256
HALF = 128
MESH = pl.DeviceIdType.MESH


def dot(a, b, dims, precision=None):
    return lax.dot_general(
        a, b, (dims, ((), ())), precision=precision, preferred_element_type=jnp.float32
    )


def split(x):
    high = x.astype(jnp.bfloat16)
    low = (x - high.astype(jnp.float32)).astype(jnp.bfloat16)
    return high, low


def factor_block(block):
    row = lax.broadcasted_iota(jnp.int32, (HALF, HALF), 0)
    lane = lax.broadcasted_iota(jnp.int32, (HALF, HALF), 1)
    sub = lax.broadcasted_iota(jnp.int32, (8, HALF), 0)
    a = block
    i = jnp.where(row == lane, 1.0, 0.0).astype(jnp.float32)
    done_a, done_i = [], []
    for k in range(0, HALF, 8):
        cols = [jnp.broadcast_to(a[:, k + j : k + j + 1], a.shape) for j in range(8)]
        head_a, head_i = a[:8], i[:8]
        mults, rows_a, rows_i = [], [], []
        for j in range(8):
            r = lax.rsqrt(cols[j][j : j + 1])
            m = cols[j] * r
            for n in range(j + 1, 8):
                cols[n] = cols[n] - m * (cols[n][j : j + 1] * r)
            row_a, row_i = head_a[j : j + 1] * r, head_i[j : j + 1] * r
            below = jnp.where(sub > j, m[:8], 0.0)
            head_a = jnp.where(sub == j, row_a, head_a - below * row_a)
            head_i = jnp.where(sub == j, row_i, head_i - below * row_i)
            mults.append(m)
            rows_a.append(row_a)
            rows_i.append(row_i)
        done_a.append(head_a)
        done_i.append(head_i)
        if k + 8 < HALF:
            a, i = a[8:], i[8:]
            for j in range(8):
                a = a - mults[j][8:] * rows_a[j]
                i = i - mults[j][8:] * rows_i[j]
    upper = jnp.where(row <= lane, jnp.concatenate(done_a, axis=0), 0.0)
    return upper, jnp.concatenate(done_i, axis=0)


def gather_kernel(gamma, own_pts, own_sketch, high, low, sketch, pts, *sems):
    count, feats = pts.shape
    own = own_sketch.shape[0]
    group = lax.axis_index("groups")
    col, core = lax.axis_index("col"), lax.axis_index("row")
    depth = lax.axis_size("col") // 2
    z, y = col // 2, lax.rem(col, 2)

    def device(z_of, y_of, core_of):
        return (group, z_of * 2 + y_of, core_of)

    def rows(z_of, y_of, core_of):
        slot = (core_of * 2 + y_of) * depth + z_of
        return pl.ds(pl.multiple_of(slot * own, 16), own)

    along_z = [device(lax.rem(z + d, depth), y, core) for d in range(1, depth)]
    y_peer, core_peer = device(z, 1 - y, core), device(z, y, 1 - core)
    barrier = pltpu.get_barrier_semaphore()
    for peer in along_z + [y_peer, core_peer]:
        pl.semaphore_signal(barrier, inc=1, device_id=peer, device_id_type=MESH)
    mine = rows(z, y, core)
    pts[mine, :] = own_pts[...]
    sketch[mine, :] = own_sketch[...]
    pl.semaphore_wait(barrier, depth + 1)

    def send(full, at, peer, number, send_sem, recv_sem):
        copy = pltpu.make_async_remote_copy(
            src_ref=full.at[at, :],
            dst_ref=full.at[at, :],
            send_sem=send_sem.at[number],
            recv_sem=recv_sem.at[number],
            device_id=peer,
            device_id_type=MESH,
        )
        copy.start()
        return copy

    arrays = [(pts, sems[0], sems[1]), (sketch, sems[2], sems[3])]
    z_copies, y_copies, c_copies = [[], []], [[], []], [[], []]
    y_base, c_base = depth - 1, 2 * depth - 1

    def first(n):
        full, ss, rs = arrays[n]
        for d in range(1, depth):
            z_copies[n].append(send(full, mine, along_z[d - 1], d - 1, ss, rs))
        y_copies[n].append(send(full, mine, y_peer, y_base, ss, rs))
        c_copies[n].append(send(full, mine, core_peer, c_base, ss, rs))

    def after_z(n, d):
        full, ss, rs = arrays[n]
        at = rows(lax.rem(z - d + depth, depth), y, core)
        z_copies[n][d - 1].wait_recv()
        y_copies[n].append(send(full, at, y_peer, y_base + d, ss, rs))
        c_copies[n].append(send(full, at, core_peer, c_base + d, ss, rs))

    def after_y(n, d):
        full, ss, rs = arrays[n]
        at = rows(lax.rem(z - d + depth, depth), 1 - y, core)
        y_copies[n][d].wait_recv()
        c_copies[n].append(send(full, at, core_peer, c_base + depth + d, ss, rs))

    first(0)
    for d in range(1, depth):
        after_z(0, d)
    first(1)
    for d in range(depth):
        after_y(0, d)
    for copy in c_copies[0]:
        copy.wait_recv()

    hops = [functools.partial(after_z, 1, d) for d in range(1, depth)]
    hops += [functools.partial(after_y, 1, d) for d in range(depth)]
    blocks = count // ROWS
    gaps = max(blocks - 1, 1)
    all_f = pts[...].astype(jnp.float32)
    ones = jnp.ones((8, feats), jnp.float32)
    all_sq = dot(ones, all_f * all_f, ((1,), (1,)), HIGHEST)[:1]
    for b in range(blocks):
        at = b * ROWS
        block = pts[at : at + ROWS, :]
        block_f = block.astype(jnp.float32)
        block_sq = jnp.sum(block_f * block_f, axis=1, keepdims=True)
        cross = dot(block, pts[...], ((1,), (1,)))
        h, l = split(jnp.exp(-gamma * (block_sq + all_sq - 2.0 * cross)))
        high[at : at + ROWS] = h
        low[at : at + ROWS] = l
        if b > 0:
            for hop in hops[(b - 1) * len(hops) // gaps : b * len(hops) // gaps]:
                hop()
    if blocks == 1:
        for hop in hops:
            hop()
    for copy in c_copies[1]:
        copy.wait_recv()
    for n in range(2):
        for copy in z_copies[n] + y_copies[n] + c_copies[n]:
            copy.wait_send()


def part_kernel(high, low, sketch, basis, factor, v, vh, vl, y, inv):
    count = high.shape[0]
    own = basis.shape[0]
    col, core = lax.axis_index("col"), lax.axis_index("row")
    me = (core * 2 + lax.rem(col, 2)) * (lax.axis_size("col") // 2) + col // 2
    v[...] = sketch[...]

    def one_pass(step, carry):
        h, l = split(v[...])
        vh[...] = h
        vl[...] = l

        def apply_rows(b, c):
            at = pl.ds(pl.multiple_of(b * ROWS, ROWS), ROWS)
            kh, kl = high[at, :], low[at, :]
            d = ((1,), (0,))
            y[at, :] = dot(kh, vh[...], d) + (dot(kh, vl[...], d) + dot(kl, vh[...], d))
            return c

        lax.fori_loop(0, count // ROWS, apply_rows, 0)
        ym = y[...]
        gram = dot(ym, ym, ((0,), (0,)), HIGHEST) / count
        u11, i11 = factor_block(gram[:HALF, :HALF])
        u12 = dot(i11, gram[:HALF, HALF:], ((1,), (0,)), HIGHEST)
        rest = gram[HALF:, HALF:] - dot(u12, u12, ((0,), (0,)), HIGHEST)
        u22, i22 = factor_block(rest)
        i21 = -dot(i22, dot(u12, i11, ((0,), (0,)), HIGHEST), ((1,), (0,)), HIGHEST)
        factor[:HALF, :HALF] = u11
        factor[:HALF, HALF:] = u12
        factor[HALF:, :HALF] = jnp.zeros_like(u11)
        factor[HALF:, HALF:] = u22
        inv[:HALF, :HALF] = i11
        inv[:HALF, HALF:] = jnp.zeros_like(i11)
        inv[HALF:, :HALF] = i21
        inv[HALF:, HALF:] = i22
        v[...] = dot(ym, inv[...], ((1,), (1,)), HIGHEST)
        return carry

    lax.fori_loop(0, PASSES + 1, one_pass, 0)
    basis[...] = v[pl.ds(pl.multiple_of(me * own, 8), own), :]


def whole_part(points, sketch):
    feats, own = points.shape
    rank = sketch.shape[1]
    count = own * lax.axis_size("col") * lax.axis_size("row")
    gamma = ((count / 32.0) ** (2.0 / feats) - 1.0) / 4.0
    copies = 2 * (lax.axis_size("col") // 2) * 2 - 1
    high, low, full = pl.pallas_call(
        functools.partial(gather_kernel, gamma),
        out_shape=(
            jax.ShapeDtypeStruct((count, count), jnp.bfloat16),
            jax.ShapeDtypeStruct((count, count), jnp.bfloat16),
            jax.ShapeDtypeStruct((count, rank), sketch.dtype),
        ),
        in_specs=[pl.BlockSpec(memory_space=pltpu.VMEM)] * 2,
        out_specs=[pl.BlockSpec(memory_space=pltpu.VMEM)] * 3,
        scratch_shapes=[pltpu.VMEM((count, feats), points.dtype)]
        + [pltpu.SemaphoreType.DMA((copies,))] * 4,
        compiler_params=pltpu.CompilerParams(
            collective_id=0, has_side_effects=True, vmem_limit_bytes=24 * 1024 * 1024
        ),
    )(points.T, sketch)
    return pl.pallas_call(
        part_kernel,
        out_shape=(
            jax.ShapeDtypeStruct((own, rank), jnp.float32),
            jax.ShapeDtypeStruct((rank, rank), jnp.float32),
        ),
        in_specs=[pl.BlockSpec(memory_space=pltpu.VMEM)] * 3,
        out_specs=[pl.BlockSpec(memory_space=pltpu.VMEM)] * 2,
        scratch_shapes=[
            pltpu.VMEM((count, rank), jnp.float32),
            pltpu.VMEM((count, rank), jnp.bfloat16),
            pltpu.VMEM((count, rank), jnp.bfloat16),
            pltpu.VMEM((count, rank), jnp.float32),
            pltpu.VMEM((rank, rank), jnp.float32),
        ],
        compiler_params=pltpu.CompilerParams(vmem_limit_bytes=28 * 1024 * 1024),
    )(high, low, full)


def kernel_rows(block_t, cols_t, gamma):
    block_f = block_t.astype(jnp.float32)
    cols_f = cols_t.astype(jnp.float32)
    block_sq = jnp.sum(block_f * block_f, axis=0)
    cols_sq = jnp.sum(cols_f * cols_f, axis=0)
    cross = lax.dot_general(
        block_t, cols_t, (((0,), (0,)), ((), ())), preferred_element_type=jnp.float32
    )
    return jnp.exp(-gamma * (block_sq[:, None] + cols_sq[None, :] - 2.0 * cross))


def orthonormal(ymat, block_count):
    local_gram = jnp.dot(ymat.T, ymat, precision=lax.Precision.HIGHEST)
    gram = lax.psum(local_gram, ("col", "row")) / block_count
    lower = jnp.linalg.cholesky(gram)
    qmat = jax.scipy.linalg.solve_triangular(lower, ymat.T, lower=True).T
    return (qmat, lower.T)


def split_part(points, sketch):
    feats, own = points.shape
    block_count = own * lax.axis_size("col") * lax.axis_size("row")
    gamma = ((block_count / 32.0) ** (2.0 / feats) - 1.0) / 4.0
    row_pts = lax.all_gather(points, "row", axis=1, tiled=True)
    col_pts = lax.all_gather(points, "col", axis=1, tiled=True)

    def tile_at():
        return kernel_rows(row_pts, col_pts, gamma)

    def accumulate_fragment(piece):
        kernel_tile = tile_at()
        return jnp.dot(
            kernel_tile, piece, precision=lax.Precision.HIGHEST, preferred_element_type=jnp.float32
        )

    def apply_operator(vector_matrix):
        running_sum = accumulate_fragment(lax.all_gather(vector_matrix, "col", axis=0, tiled=True))
        return lax.psum_scatter(running_sum, "row", scatter_dimension=0, tiled=True)

    ymat = apply_operator(sketch)
    for step in range(PASSES):
        qmat, upper = orthonormal(ymat, block_count)
        ymat = apply_operator(qmat)
    basis, factor = orthonormal(ymat, block_count)
    return (basis, factor)


def local(points, sketch):
    count = points.shape[1] * lax.axis_size("col") * lax.axis_size("row")
    small = count <= MAX_POINTS and count % ROWS == 0
    pairs = lax.axis_size("col") % 2 == 0 and lax.axis_size("row") == 2
    if small and pairs and sketch.shape[1] == 2 * HALF and points.shape[1] % 16 == 0:
        return whole_part(points, sketch)
    return split_part(points, sketch)


def solution(mesh):
    in_specs = (P(None, ("groups", "col", "row")), P(("groups", "col", "row"), None))
    out_specs = (P(("groups", "col", "row"), None), P("groups", None))
    return jax.shard_map(local, mesh=mesh, in_specs=in_specs, out_specs=out_specs, check_vma=False)
```

```python
import functools

import jax
import jax.numpy as jnp
from jax import lax
from jax.experimental import pallas as pl
from jax.experimental.pallas import tpu as pltpu
from jax.sharding import PartitionSpec as P

PASSES = 2
HIGHEST = lax.Precision.HIGHEST
MAX_POINTS = 2048
ROWS = 256
HALF = 128
MESH = pl.DeviceIdType.MESH


def dot(a, b, dims, precision=None):
    return lax.dot_general(
        a, b, (dims, ((), ())), precision=precision, preferred_element_type=jnp.float32
    )


def split(x):
    high = x.astype(jnp.bfloat16)
    low = (x - high.astype(jnp.float32)).astype(jnp.bfloat16)
    return high, low


def factor_block(block):
    row = lax.broadcasted_iota(jnp.int32, (HALF, HALF), 0)
    lane = lax.broadcasted_iota(jnp.int32, (HALF, HALF), 1)
    sub = lax.broadcasted_iota(jnp.int32, (8, HALF), 0)
    a = block
    i = jnp.where(row == lane, 1.0, 0.0).astype(jnp.float32)
    done_a, done_i = [], []
    for k in range(0, HALF, 8):
        cols = [jnp.broadcast_to(a[:, k + j : k + j + 1], a.shape) for j in range(8)]
        head_a, head_i = a[:8], i[:8]
        mults, rows_a, rows_i = [], [], []
        for j in range(8):
            r = lax.rsqrt(cols[j][j : j + 1])
            m = cols[j] * r
            for n in range(j + 1, 8):
                cols[n] = cols[n] - m * (cols[n][j : j + 1] * r)
            row_a, row_i = head_a[j : j + 1] * r, head_i[j : j + 1] * r
            below = jnp.where(sub > j, m[:8], 0.0)
            head_a = jnp.where(sub == j, row_a, head_a - below * row_a)
            head_i = jnp.where(sub == j, row_i, head_i - below * row_i)
            mults.append(m)
            rows_a.append(row_a)
            rows_i.append(row_i)
        done_a.append(head_a)
        done_i.append(head_i)
        if k + 8 < HALF:
            a, i = a[8:], i[8:]
            for j in range(8):
                a = a - mults[j][8:] * rows_a[j]
                i = i - mults[j][8:] * rows_i[j]
    upper = jnp.where(row <= lane, jnp.concatenate(done_a, axis=0), 0.0)
    return upper, jnp.concatenate(done_i, axis=0)


def gather_kernel(gamma, own_pts, own_sketch, high, low, sketch, pts, *sems):
    count, feats = pts.shape
    own = own_sketch.shape[0]
    group = lax.axis_index("groups")
    col, core = lax.axis_index("col"), lax.axis_index("row")
    depth = lax.axis_size("col") // 2
    z, y = col // 2, lax.rem(col, 2)

    def device(z_of, y_of, core_of):
        return (group, z_of * 2 + y_of, core_of)

    def rows(z_of, y_of, core_of):
        slot = (core_of * 2 + y_of) * depth + z_of
        return pl.ds(pl.multiple_of(slot * own, 16), own)

    along_z = [device(lax.rem(z + d, depth), y, core) for d in range(1, depth)]
    y_peer, core_peer = device(z, 1 - y, core), device(z, y, 1 - core)
    barrier = pltpu.get_barrier_semaphore()
    for peer in along_z + [y_peer, core_peer]:
        pl.semaphore_signal(barrier, inc=1, device_id=peer, device_id_type=MESH)
    mine = rows(z, y, core)
    pts[mine, :] = own_pts[...]
    sketch[mine, :] = own_sketch[...]
    pl.semaphore_wait(barrier, depth + 1)

    def send(full, at, peer, number, send_sem, recv_sem):
        copy = pltpu.make_async_remote_copy(
            src_ref=full.at[at, :],
            dst_ref=full.at[at, :],
            send_sem=send_sem.at[number],
            recv_sem=recv_sem.at[number],
            device_id=peer,
            device_id_type=MESH,
        )
        copy.start()
        return copy

    arrays = [(pts, sems[0], sems[1]), (sketch, sems[2], sems[3])]
    z_copies, y_copies, c_copies = [[], []], [[], []], [[], []]
    y_base, c_base = depth - 1, 2 * depth - 1

    def first(n):
        full, ss, rs = arrays[n]
        for d in range(1, depth):
            z_copies[n].append(send(full, mine, along_z[d - 1], d - 1, ss, rs))
        y_copies[n].append(send(full, mine, y_peer, y_base, ss, rs))
        c_copies[n].append(send(full, mine, core_peer, c_base, ss, rs))

    def after_z(n, d):
        full, ss, rs = arrays[n]
        at = rows(lax.rem(z - d + depth, depth), y, core)
        z_copies[n][d - 1].wait_recv()
        y_copies[n].append(send(full, at, y_peer, y_base + d, ss, rs))
        c_copies[n].append(send(full, at, core_peer, c_base + d, ss, rs))

    def after_y(n, d):
        full, ss, rs = arrays[n]
        at = rows(lax.rem(z - d + depth, depth), 1 - y, core)
        y_copies[n][d].wait_recv()
        c_copies[n].append(send(full, at, core_peer, c_base + depth + d, ss, rs))

    first(0)
    first(1)
    for d in range(1, depth):
        after_z(0, d)
    for d in range(depth):
        after_y(0, d)
    for copy in c_copies[0]:
        copy.wait_recv()

    hops = [functools.partial(after_z, 1, d) for d in range(1, depth)]
    hops += [functools.partial(after_y, 1, d) for d in range(depth)]
    blocks = count // ROWS
    gaps = max(blocks - 1, 1)
    all_f = pts[...].astype(jnp.float32)
    ones = jnp.ones((8, feats), jnp.float32)
    all_sq = dot(ones, all_f * all_f, ((1,), (1,)), HIGHEST)[:1]
    for b in range(blocks):
        at = b * ROWS
        block = pts[at : at + ROWS, :]
        block_f = block.astype(jnp.float32)
        block_sq = jnp.sum(block_f * block_f, axis=1, keepdims=True)
        cross = dot(block, pts[...], ((1,), (1,)))
        h, l = split(jnp.exp(-gamma * (block_sq + all_sq - 2.0 * cross)))
        high[at : at + ROWS] = h
        low[at : at + ROWS] = l
        if b > 0:
            for hop in hops[(b - 1) * len(hops) // gaps : b * len(hops) // gaps]:
                hop()
    if blocks == 1:
        for hop in hops:
            hop()
    for copy in c_copies[1]:
        copy.wait_recv()
    for n in range(2):
        for copy in z_copies[n] + y_copies[n] + c_copies[n]:
            copy.wait_send()


def part_kernel(high, low, sketch, basis, factor, v, vh, vl, y, inv):
    count = high.shape[0]
    own = basis.shape[0]
    col, core = lax.axis_index("col"), lax.axis_index("row")
    me = (core * 2 + lax.rem(col, 2)) * (lax.axis_size("col") // 2) + col // 2
    v[...] = sketch[...]

    def one_pass(step, carry):
        h, l = split(v[...])
        vh[...] = h
        vl[...] = l

        def apply_rows(b, c):
            at = pl.ds(pl.multiple_of(b * ROWS, ROWS), ROWS)
            kh, kl = high[at, :], low[at, :]
            d = ((1,), (0,))
            y[at, :] = dot(kh, vh[...], d) + (dot(kh, vl[...], d) + dot(kl, vh[...], d))
            return c

        lax.fori_loop(0, count // ROWS, apply_rows, 0)
        ym = y[...]
        h, l = split(ym)
        vh[...] = h
        vl[...] = l
        d = ((0,), (0,))
        cross = dot(vh[...], vl[...], d)
        gram = dot(vh[...], vh[...], d) + (cross + cross.T + dot(vl[...], vl[...], d))
        gram = gram / count
        u11, i11 = factor_block(gram[:HALF, :HALF])
        u12 = dot(i11, gram[:HALF, HALF:], ((1,), (0,)), HIGHEST)
        rest = gram[HALF:, HALF:] - dot(u12, u12, ((0,), (0,)), HIGHEST)
        u22, i22 = factor_block(rest)
        i21 = -dot(i22, dot(u12, i11, ((0,), (0,)), HIGHEST), ((1,), (0,)), HIGHEST)
        factor[:HALF, :HALF] = u11
        factor[:HALF, HALF:] = u12
        factor[HALF:, :HALF] = jnp.zeros_like(u11)
        factor[HALF:, HALF:] = u22
        inv[:HALF, :HALF] = i11
        inv[:HALF, HALF:] = jnp.zeros_like(i11)
        inv[HALF:, :HALF] = i21
        inv[HALF:, HALF:] = i22

        @pl.when(step < PASSES)
        def _():
            v[...] = dot(y[...], inv[...], ((1,), (1,)), HIGHEST)

        return carry

    lax.fori_loop(0, PASSES + 1, one_pass, 0)
    mine = y[pl.ds(pl.multiple_of(me * own, 8), own), :]
    basis[...] = dot(mine, inv[...], ((1,), (1,)), HIGHEST)


def whole_part(points, sketch):
    feats, own = points.shape
    rank = sketch.shape[1]
    count = own * lax.axis_size("col") * lax.axis_size("row")
    gamma = ((count / 32.0) ** (2.0 / feats) - 1.0) / 4.0
    copies = 2 * (lax.axis_size("col") // 2) * 2 - 1
    high, low, full = pl.pallas_call(
        functools.partial(gather_kernel, gamma),
        out_shape=(
            jax.ShapeDtypeStruct((count, count), jnp.bfloat16),
            jax.ShapeDtypeStruct((count, count), jnp.bfloat16),
            jax.ShapeDtypeStruct((count, rank), sketch.dtype),
        ),
        in_specs=[pl.BlockSpec(memory_space=pltpu.VMEM)] * 2,
        out_specs=[pl.BlockSpec(memory_space=pltpu.VMEM)] * 3,
        scratch_shapes=[pltpu.VMEM((count, feats), points.dtype)]
        + [pltpu.SemaphoreType.DMA((copies,))] * 4,
        compiler_params=pltpu.CompilerParams(
            collective_id=0, has_side_effects=True, vmem_limit_bytes=24 * 1024 * 1024
        ),
    )(points.T, sketch)
    return pl.pallas_call(
        part_kernel,
        out_shape=(
            jax.ShapeDtypeStruct((own, rank), jnp.float32),
            jax.ShapeDtypeStruct((rank, rank), jnp.float32),
        ),
        in_specs=[pl.BlockSpec(memory_space=pltpu.VMEM)] * 3,
        out_specs=[pl.BlockSpec(memory_space=pltpu.VMEM)] * 2,
        scratch_shapes=[
            pltpu.VMEM((count, rank), jnp.float32),
            pltpu.VMEM((count, rank), jnp.bfloat16),
            pltpu.VMEM((count, rank), jnp.bfloat16),
            pltpu.VMEM((count, rank), jnp.float32),
            pltpu.VMEM((rank, rank), jnp.float32),
        ],
        compiler_params=pltpu.CompilerParams(vmem_limit_bytes=28 * 1024 * 1024),
    )(high, low, full)


def kernel_rows(block_t, cols_t, gamma):
    block_f = block_t.astype(jnp.float32)
    cols_f = cols_t.astype(jnp.float32)
    block_sq = jnp.sum(block_f * block_f, axis=0)
    cols_sq = jnp.sum(cols_f * cols_f, axis=0)
    cross = lax.dot_general(
        block_t, cols_t, (((0,), (0,)), ((), ())), preferred_element_type=jnp.float32
    )
    return jnp.exp(-gamma * (block_sq[:, None] + cols_sq[None, :] - 2.0 * cross))


def orthonormal(ymat, block_count):
    local_gram = jnp.dot(ymat.T, ymat, precision=lax.Precision.HIGHEST)
    gram = lax.psum(local_gram, ("col", "row")) / block_count
    lower = jnp.linalg.cholesky(gram)
    qmat = jax.scipy.linalg.solve_triangular(lower, ymat.T, lower=True).T
    return (qmat, lower.T)


def split_part(points, sketch):
    feats, own = points.shape
    block_count = own * lax.axis_size("col") * lax.axis_size("row")
    gamma = ((block_count / 32.0) ** (2.0 / feats) - 1.0) / 4.0
    row_pts = lax.all_gather(points, "row", axis=1, tiled=True)
    col_pts = lax.all_gather(points, "col", axis=1, tiled=True)

    def tile_at():
        return kernel_rows(row_pts, col_pts, gamma)

    def accumulate_fragment(piece):
        kernel_tile = tile_at()
        return jnp.dot(
            kernel_tile, piece, precision=lax.Precision.HIGHEST, preferred_element_type=jnp.float32
        )

    def apply_operator(vector_matrix):
        running_sum = accumulate_fragment(lax.all_gather(vector_matrix, "col", axis=0, tiled=True))
        return lax.psum_scatter(running_sum, "row", scatter_dimension=0, tiled=True)

    ymat = apply_operator(sketch)
    for step in range(PASSES):
        qmat, upper = orthonormal(ymat, block_count)
        ymat = apply_operator(qmat)
    basis, factor = orthonormal(ymat, block_count)
    return (basis, factor)


def local(points, sketch):
    count = points.shape[1] * lax.axis_size("col") * lax.axis_size("row")
    small = count <= MAX_POINTS and count % ROWS == 0
    pairs = lax.axis_size("col") % 2 == 0 and lax.axis_size("row") == 2
    if small and pairs and sketch.shape[1] == 2 * HALF and points.shape[1] % 16 == 0:
        return whole_part(points, sketch)
    return split_part(points, sketch)


def solution(mesh):
    in_specs = (P(None, ("groups", "col", "row")), P(("groups", "col", "row"), None))
    out_specs = (P(("groups", "col", "row"), None), P("groups", None))
    return jax.shard_map(local, mesh=mesh, in_specs=in_specs, out_specs=out_specs, check_vma=False)
```

```python
import functools

import jax
import jax.numpy as jnp
from jax import lax
from jax.experimental import pallas as pl
from jax.experimental.pallas import tpu as pltpu
from jax.sharding import PartitionSpec as P

PASSES = 2
HIGHEST = lax.Precision.HIGHEST
MAX_POINTS = 2048
ROWS = 256
HALF = 128
MESH = pl.DeviceIdType.MESH


def dot(a, b, dims, precision=None):
    return lax.dot_general(
        a, b, (dims, ((), ())), precision=precision, preferred_element_type=jnp.float32
    )


def split(x):
    high = x.astype(jnp.bfloat16)
    low = (x - high.astype(jnp.float32)).astype(jnp.bfloat16)
    return high, low


def factor_block(block):
    row = lax.broadcasted_iota(jnp.int32, (HALF, HALF), 0)
    lane = lax.broadcasted_iota(jnp.int32, (HALF, HALF), 1)
    sub = lax.broadcasted_iota(jnp.int32, (8, HALF), 0)
    a = block
    i = jnp.where(row == lane, 1.0, 0.0).astype(jnp.float32)
    done_a, done_i = [], []
    for k in range(0, HALF, 8):
        cols = [jnp.broadcast_to(a[:, k + j : k + j + 1], a.shape) for j in range(8)]
        head_a, head_i = a[:8], i[:8]
        mults, rows_a, rows_i = [], [], []
        for j in range(8):
            r = lax.rsqrt(cols[j][j : j + 1])
            m = cols[j] * r
            for n in range(j + 1, 8):
                cols[n] = cols[n] - m * (cols[n][j : j + 1] * r)
            row_a, row_i = head_a[j : j + 1] * r, head_i[j : j + 1] * r
            below = jnp.where(sub > j, m[:8], 0.0)
            head_a = jnp.where(sub == j, row_a, head_a - below * row_a)
            head_i = jnp.where(sub == j, row_i, head_i - below * row_i)
            mults.append(m)
            rows_a.append(row_a)
            rows_i.append(row_i)
        done_a.append(head_a)
        done_i.append(head_i)
        if k + 8 < HALF:
            a, i = a[8:], i[8:]
            for j in range(8):
                a = a - mults[j][8:] * rows_a[j]
                i = i - mults[j][8:] * rows_i[j]
    upper = jnp.where(row <= lane, jnp.concatenate(done_a, axis=0), 0.0)
    return upper, jnp.concatenate(done_i, axis=0)


def gather_kernel(gamma, own_pts, own_sketch, high, low, sketch, pts, *sems):
    count, feats = pts.shape
    own = own_sketch.shape[0]
    group = lax.axis_index("groups")
    col, core = lax.axis_index("col"), lax.axis_index("row")
    depth = lax.axis_size("col") // 2
    z, y = col // 2, lax.rem(col, 2)

    def device(z_of, y_of, core_of):
        return (group, z_of * 2 + y_of, core_of)

    def rows(z_of, y_of, core_of):
        slot = (core_of * 2 + y_of) * depth + z_of
        return pl.ds(pl.multiple_of(slot * own, 16), own)

    along_z = [device(lax.rem(z + d, depth), y, core) for d in range(1, depth)]
    y_peer, core_peer = device(z, 1 - y, core), device(z, y, 1 - core)
    barrier = pltpu.get_barrier_semaphore()
    for peer in along_z + [y_peer, core_peer]:
        pl.semaphore_signal(barrier, inc=1, device_id=peer, device_id_type=MESH)
    mine = rows(z, y, core)
    pts[mine, :] = own_pts[...]
    sketch[mine, :] = own_sketch[...]
    pl.semaphore_wait(barrier, depth + 1)

    def send(full, at, peer, number, send_sem, recv_sem):
        copy = pltpu.make_async_remote_copy(
            src_ref=full.at[at, :],
            dst_ref=full.at[at, :],
            send_sem=send_sem.at[number],
            recv_sem=recv_sem.at[number],
            device_id=peer,
            device_id_type=MESH,
        )
        copy.start()
        return copy

    arrays = [(pts, sems[0], sems[1]), (sketch, sems[2], sems[3])]
    z_copies, y_copies, c_copies = [[], []], [[], []], [[], []]
    y_base, c_base = depth - 1, 2 * depth - 1

    def first(n):
        full, ss, rs = arrays[n]
        for d in range(1, depth):
            z_copies[n].append(send(full, mine, along_z[d - 1], d - 1, ss, rs))
        y_copies[n].append(send(full, mine, y_peer, y_base, ss, rs))
        c_copies[n].append(send(full, mine, core_peer, c_base, ss, rs))

    def after_z(n, d):
        full, ss, rs = arrays[n]
        at = rows(lax.rem(z - d + depth, depth), y, core)
        z_copies[n][d - 1].wait_recv()
        y_copies[n].append(send(full, at, y_peer, y_base + d, ss, rs))
        c_copies[n].append(send(full, at, core_peer, c_base + d, ss, rs))

    def after_y(n, d):
        full, ss, rs = arrays[n]
        at = rows(lax.rem(z - d + depth, depth), 1 - y, core)
        y_copies[n][d].wait_recv()
        c_copies[n].append(send(full, at, core_peer, c_base + depth + d, ss, rs))

    first(0)
    for d in range(1, depth):
        after_z(0, d)
    first(1)
    for d in range(depth):
        after_y(0, d)
    for copy in c_copies[0]:
        copy.wait_recv()

    hops = [functools.partial(after_z, 1, d) for d in range(1, depth)]
    hops += [functools.partial(after_y, 1, d) for d in range(depth)]
    blocks = count // ROWS
    gaps = max(blocks - 1, 1)
    all_f = pts[...].astype(jnp.float32)
    ones = jnp.ones((8, feats), jnp.float32)
    all_sq = dot(ones, all_f * all_f, ((1,), (1,)), HIGHEST)[:1]
    for b in range(blocks):
        at = b * ROWS
        block = pts[at : at + ROWS, :]
        block_f = block.astype(jnp.float32)
        block_sq = jnp.sum(block_f * block_f, axis=1, keepdims=True)
        cross = dot(block, pts[...], ((1,), (1,)))
        h, l = split(jnp.exp(-gamma * (block_sq + all_sq - 2.0 * cross)))
        high[at : at + ROWS] = h
        low[at : at + ROWS] = l
        if b > 0:
            for hop in hops[(b - 1) * len(hops) // gaps : b * len(hops) // gaps]:
                hop()
    if blocks == 1:
        for hop in hops:
            hop()
    for copy in c_copies[1]:
        copy.wait_recv()
    for n in range(2):
        for copy in z_copies[n] + y_copies[n] + c_copies[n]:
            copy.wait_send()


def part_kernel(high, low, sketch, basis, factor, vh, vl, y, inv):
    count = high.shape[0]
    own = basis.shape[0]
    col, core = lax.axis_index("col"), lax.axis_index("row")
    me = (core * 2 + lax.rem(col, 2)) * (lax.axis_size("col") // 2) + col // 2
    h, l = split(sketch[...])
    vh[...] = h
    vl[...] = l

    def one_pass(step, carry):
        def apply_rows(b, c):
            at = pl.ds(pl.multiple_of(b * ROWS, ROWS), ROWS)
            kh, kl = high[at, :], low[at, :]
            d = ((1,), (0,))
            y[at, :] = dot(kh, vh[...], d) + (dot(kh, vl[...], d) + dot(kl, vh[...], d))
            return c

        lax.fori_loop(0, count // ROWS, apply_rows, 0)
        ym = y[...]
        h, l = split(ym)
        vh[...] = h
        vl[...] = l
        d = ((0,), (0,))
        cross = dot(vh[...], vl[...], d)
        gram = dot(vh[...], vh[...], d) + (cross + cross.T + dot(vl[...], vl[...], d))
        gram = gram / count
        u11, i11 = factor_block(gram[:HALF, :HALF])
        u12 = dot(i11, gram[:HALF, HALF:], ((1,), (0,)), HIGHEST)
        rest = gram[HALF:, HALF:] - dot(u12, u12, ((0,), (0,)), HIGHEST)
        u22, i22 = factor_block(rest)
        i21 = -dot(i22, dot(u12, i11, ((0,), (0,)), HIGHEST), ((1,), (0,)), HIGHEST)
        factor[:HALF, :HALF] = u11
        factor[:HALF, HALF:] = u12
        factor[HALF:, :HALF] = jnp.zeros_like(u11)
        factor[HALF:, HALF:] = u22
        inv[:HALF, :HALF] = i11
        inv[:HALF, HALF:] = jnp.zeros_like(i11)
        inv[HALF:, :HALF] = i21
        inv[HALF:, HALF:] = i22

        @pl.when(step < PASSES)
        def _():
            h, l = split(dot(y[...], inv[...], ((1,), (1,)), HIGHEST))
            vh[...] = h
            vl[...] = l

        return carry

    lax.fori_loop(0, PASSES + 1, one_pass, 0)
    mine = y[pl.ds(pl.multiple_of(me * own, 8), own), :]
    basis[...] = dot(mine, inv[...], ((1,), (1,)), HIGHEST)


def whole_part(points, sketch):
    feats, own = points.shape
    rank = sketch.shape[1]
    count = own * lax.axis_size("col") * lax.axis_size("row")
    gamma = ((count / 32.0) ** (2.0 / feats) - 1.0) / 4.0
    copies = 2 * (lax.axis_size("col") // 2) * 2 - 1
    high, low, full = pl.pallas_call(
        functools.partial(gather_kernel, gamma),
        out_shape=(
            jax.ShapeDtypeStruct((count, count), jnp.bfloat16),
            jax.ShapeDtypeStruct((count, count), jnp.bfloat16),
            jax.ShapeDtypeStruct((count, rank), sketch.dtype),
        ),
        in_specs=[pl.BlockSpec(memory_space=pltpu.VMEM)] * 2,
        out_specs=[pl.BlockSpec(memory_space=pltpu.VMEM)] * 3,
        scratch_shapes=[pltpu.VMEM((count, feats), points.dtype)]
        + [pltpu.SemaphoreType.DMA((copies,))] * 4,
        compiler_params=pltpu.CompilerParams(
            collective_id=0, has_side_effects=True, vmem_limit_bytes=24 * 1024 * 1024
        ),
    )(points.T, sketch)
    return pl.pallas_call(
        part_kernel,
        out_shape=(
            jax.ShapeDtypeStruct((own, rank), jnp.float32),
            jax.ShapeDtypeStruct((rank, rank), jnp.float32),
        ),
        in_specs=[pl.BlockSpec(memory_space=pltpu.VMEM)] * 3,
        out_specs=[pl.BlockSpec(memory_space=pltpu.VMEM)] * 2,
        scratch_shapes=[
            pltpu.VMEM((count, rank), jnp.bfloat16),
            pltpu.VMEM((count, rank), jnp.bfloat16),
            pltpu.VMEM((count, rank), jnp.float32),
            pltpu.VMEM((rank, rank), jnp.float32),
        ],
        compiler_params=pltpu.CompilerParams(vmem_limit_bytes=28 * 1024 * 1024),
    )(high, low, full)


def kernel_rows(block_t, cols_t, gamma):
    block_f = block_t.astype(jnp.float32)
    cols_f = cols_t.astype(jnp.float32)
    block_sq = jnp.sum(block_f * block_f, axis=0)
    cols_sq = jnp.sum(cols_f * cols_f, axis=0)
    cross = lax.dot_general(
        block_t, cols_t, (((0,), (0,)), ((), ())), preferred_element_type=jnp.float32
    )
    return jnp.exp(-gamma * (block_sq[:, None] + cols_sq[None, :] - 2.0 * cross))


def orthonormal(ymat, block_count):
    local_gram = jnp.dot(ymat.T, ymat, precision=lax.Precision.HIGHEST)
    gram = lax.psum(local_gram, ("col", "row")) / block_count
    lower = jnp.linalg.cholesky(gram)
    qmat = jax.scipy.linalg.solve_triangular(lower, ymat.T, lower=True).T
    return (qmat, lower.T)


def split_part(points, sketch):
    feats, own = points.shape
    block_count = own * lax.axis_size("col") * lax.axis_size("row")
    gamma = ((block_count / 32.0) ** (2.0 / feats) - 1.0) / 4.0
    row_pts = lax.all_gather(points, "row", axis=1, tiled=True)
    col_pts = lax.all_gather(points, "col", axis=1, tiled=True)

    def tile_at():
        return kernel_rows(row_pts, col_pts, gamma)

    def accumulate_fragment(piece):
        kernel_tile = tile_at()
        return jnp.dot(
            kernel_tile, piece, precision=lax.Precision.HIGHEST, preferred_element_type=jnp.float32
        )

    def apply_operator(vector_matrix):
        running_sum = accumulate_fragment(lax.all_gather(vector_matrix, "col", axis=0, tiled=True))
        return lax.psum_scatter(running_sum, "row", scatter_dimension=0, tiled=True)

    ymat = apply_operator(sketch)
    for step in range(PASSES):
        qmat, upper = orthonormal(ymat, block_count)
        ymat = apply_operator(qmat)
    basis, factor = orthonormal(ymat, block_count)
    return (basis, factor)


def local(points, sketch):
    count = points.shape[1] * lax.axis_size("col") * lax.axis_size("row")
    small = count <= MAX_POINTS and count % ROWS == 0
    pairs = lax.axis_size("col") % 2 == 0 and lax.axis_size("row") == 2
    if small and pairs and sketch.shape[1] == 2 * HALF and points.shape[1] % 16 == 0:
        return whole_part(points, sketch)
    return split_part(points, sketch)


def solution(mesh):
    in_specs = (P(None, ("groups", "col", "row")), P(("groups", "col", "row"), None))
    out_specs = (P(("groups", "col", "row"), None), P("groups", None))
    return jax.shard_map(local, mesh=mesh, in_specs=in_specs, out_specs=out_specs, check_vma=False)
```

```python
import functools

import jax
import jax.numpy as jnp
from jax import lax
from jax.experimental import pallas as pl
from jax.experimental.pallas import tpu as pltpu
from jax.sharding import PartitionSpec as P

PASSES = 2
HIGHEST = lax.Precision.HIGHEST
MAX_POINTS = 2048
ROWS = 256
HALF = 128
MESH = pl.DeviceIdType.MESH


def dot(a, b, dims, precision=None):
    return lax.dot_general(
        a, b, (dims, ((), ())), precision=precision, preferred_element_type=jnp.float32
    )


def split(x):
    high = x.astype(jnp.bfloat16)
    low = (x - high.astype(jnp.float32)).astype(jnp.bfloat16)
    return high, low


def factor_block(block):
    row = lax.broadcasted_iota(jnp.int32, (HALF, HALF), 0)
    lane = lax.broadcasted_iota(jnp.int32, (HALF, HALF), 1)
    sub = lax.broadcasted_iota(jnp.int32, (8, HALF), 0)
    a = block
    i = jnp.where(row == lane, 1.0, 0.0).astype(jnp.float32)
    done_a, done_i = [], []
    for k in range(0, HALF, 8):
        cols = [jnp.broadcast_to(a[:, k + j : k + j + 1], a.shape) for j in range(8)]
        head_a, head_i = a[:8], i[:8]
        mults, rows_a, rows_i = [], [], []
        for j in range(8):
            r = lax.rsqrt(cols[j][j : j + 1])
            m = cols[j] * r
            for n in range(j + 1, 8):
                cols[n] = cols[n] - m * (cols[n][j : j + 1] * r)
            row_a, row_i = head_a[j : j + 1] * r, head_i[j : j + 1] * r
            below = jnp.where(sub > j, m[:8], 0.0)
            head_a = jnp.where(sub == j, row_a, head_a - below * row_a)
            head_i = jnp.where(sub == j, row_i, head_i - below * row_i)
            mults.append(m)
            rows_a.append(row_a)
            rows_i.append(row_i)
        done_a.append(head_a)
        done_i.append(head_i)
        if k + 8 < HALF:
            a, i = a[8:], i[8:]
            for j in range(8):
                a = a - mults[j][8:] * rows_a[j]
                i = i - mults[j][8:] * rows_i[j]
    upper = jnp.where(row <= lane, jnp.concatenate(done_a, axis=0), 0.0)
    return upper, jnp.concatenate(done_i, axis=0)


def gather_kernel(gamma, own_pts, own_sketch, high, low, sketch, pts, *sems):
    count, feats = pts.shape
    own = own_sketch.shape[0]
    group = lax.axis_index("groups")
    col, core = lax.axis_index("col"), lax.axis_index("row")
    depth = lax.axis_size("col") // 2
    z, y = col // 2, lax.rem(col, 2)

    def device(z_of, y_of, core_of):
        return (group, z_of * 2 + y_of, core_of)

    def rows(z_of, y_of, core_of):
        slot = (core_of * 2 + y_of) * depth + z_of
        return pl.ds(pl.multiple_of(slot * own, 16), own)

    along_z = [device(lax.rem(z + d, depth), y, core) for d in range(1, depth)]
    y_peer, core_peer = device(z, 1 - y, core), device(z, y, 1 - core)
    barrier = pltpu.get_barrier_semaphore()
    for peer in along_z + [y_peer, core_peer]:
        pl.semaphore_signal(barrier, inc=1, device_id=peer, device_id_type=MESH)
    mine = rows(z, y, core)
    pts[mine, :] = own_pts[...]
    sketch[mine, :] = own_sketch[...]
    pl.semaphore_wait(barrier, depth + 1)

    def send(full, at, peer, number, send_sem, recv_sem):
        copy = pltpu.make_async_remote_copy(
            src_ref=full.at[at, :],
            dst_ref=full.at[at, :],
            send_sem=send_sem.at[number],
            recv_sem=recv_sem.at[number],
            device_id=peer,
            device_id_type=MESH,
        )
        copy.start()
        return copy

    arrays = [(pts, sems[0], sems[1]), (sketch, sems[2], sems[3])]
    z_copies, y_copies, c_copies = [[], []], [[], []], [[], []]
    y_base, c_base = depth - 1, 2 * depth - 1

    def first(n):
        full, ss, rs = arrays[n]
        for d in range(1, depth):
            z_copies[n].append(send(full, mine, along_z[d - 1], d - 1, ss, rs))
        y_copies[n].append(send(full, mine, y_peer, y_base, ss, rs))
        c_copies[n].append(send(full, mine, core_peer, c_base, ss, rs))

    def after_z(n, d):
        full, ss, rs = arrays[n]
        at = rows(lax.rem(z - d + depth, depth), y, core)
        z_copies[n][d - 1].wait_recv()
        y_copies[n].append(send(full, at, y_peer, y_base + d, ss, rs))
        c_copies[n].append(send(full, at, core_peer, c_base + d, ss, rs))

    def after_y(n, d):
        full, ss, rs = arrays[n]
        at = rows(lax.rem(z - d + depth, depth), 1 - y, core)
        y_copies[n][d].wait_recv()
        c_copies[n].append(send(full, at, core_peer, c_base + depth + d, ss, rs))

    first(0)
    for d in range(1, depth):
        after_z(0, d)
    first(1)
    for d in range(depth):
        after_y(0, d)
    for copy in c_copies[0]:
        copy.wait_recv()

    hops = [functools.partial(after_z, 1, d) for d in range(1, depth)]
    hops += [functools.partial(after_y, 1, d) for d in range(depth)]
    blocks = count // ROWS
    gaps = max(blocks - 1, 1)
    all_f = pts[...].astype(jnp.float32)
    ones = jnp.ones((8, feats), jnp.float32)
    all_sq = dot(ones, all_f * all_f, ((1,), (1,)), HIGHEST)[:1]
    for b in range(blocks):
        at = b * ROWS
        block = pts[at : at + ROWS, :]
        block_f = block.astype(jnp.float32)
        block_sq = jnp.sum(block_f * block_f, axis=1, keepdims=True)
        cross = dot(block, pts[...], ((1,), (1,)))
        h, l = split(jnp.exp(-gamma * (block_sq + all_sq - 2.0 * cross)))
        high[at : at + ROWS] = h
        low[at : at + ROWS] = l
        if b > 0:
            for hop in hops[(b - 1) * len(hops) // gaps : b * len(hops) // gaps]:
                hop()
    if blocks == 1:
        for hop in hops:
            hop()
    for copy in c_copies[1]:
        copy.wait_recv()
    for n in range(2):
        for copy in z_copies[n] + y_copies[n] + c_copies[n]:
            copy.wait_send()


def part_kernel(high, low, sketch, basis, factor, vh, vl, y, inv):
    count = high.shape[0]
    size = 2 * ROWS if count % (2 * ROWS) == 0 else ROWS
    own = basis.shape[0]
    col, core = lax.axis_index("col"), lax.axis_index("row")
    me = (core * 2 + lax.rem(col, 2)) * (lax.axis_size("col") // 2) + col // 2
    h, l = split(sketch[...])
    vh[...] = h
    vl[...] = l

    def one_pass(step, carry):
        def apply_rows(b, c):
            at = pl.ds(pl.multiple_of(b * size, size), size)
            kh, kl = high[at, :], low[at, :]
            d = ((1,), (0,))
            y[at, :] = dot(kh, vh[...], d) + (dot(kh, vl[...], d) + dot(kl, vh[...], d))
            return c

        lax.fori_loop(0, count // size, apply_rows, 0)
        ym = y[...]
        h, l = split(ym)
        vh[...] = h
        vl[...] = l
        d = ((0,), (0,))
        cross = dot(vh[...], vl[...], d)
        gram = dot(vh[...], vh[...], d) + (cross + cross.T + dot(vl[...], vl[...], d))
        gram = gram / count
        u11, i11 = factor_block(gram[:HALF, :HALF])
        u12 = dot(i11, gram[:HALF, HALF:], ((1,), (0,)), HIGHEST)
        rest = gram[HALF:, HALF:] - dot(u12, u12, ((0,), (0,)), HIGHEST)
        u22, i22 = factor_block(rest)
        i21 = -dot(i22, dot(u12, i11, ((0,), (0,)), HIGHEST), ((1,), (0,)), HIGHEST)
        factor[:HALF, :HALF] = u11
        factor[:HALF, HALF:] = u12
        factor[HALF:, :HALF] = jnp.zeros_like(u11)
        factor[HALF:, HALF:] = u22
        inv[:HALF, :HALF] = i11
        inv[:HALF, HALF:] = jnp.zeros_like(i11)
        inv[HALF:, :HALF] = i21
        inv[HALF:, HALF:] = i22

        @pl.when(step < PASSES)
        def _():
            h, l = split(dot(y[...], inv[...], ((1,), (1,)), HIGHEST))
            vh[...] = h
            vl[...] = l

        return carry

    lax.fori_loop(0, PASSES + 1, one_pass, 0)
    mine = y[pl.ds(pl.multiple_of(me * own, 8), own), :]
    basis[...] = dot(mine, inv[...], ((1,), (1,)), HIGHEST)


def whole_part(points, sketch):
    feats, own = points.shape
    rank = sketch.shape[1]
    count = own * lax.axis_size("col") * lax.axis_size("row")
    gamma = ((count / 32.0) ** (2.0 / feats) - 1.0) / 4.0
    copies = 2 * (lax.axis_size("col") // 2) * 2 - 1
    high, low, full = pl.pallas_call(
        functools.partial(gather_kernel, gamma),
        out_shape=(
            jax.ShapeDtypeStruct((count, count), jnp.bfloat16),
            jax.ShapeDtypeStruct((count, count), jnp.bfloat16),
            jax.ShapeDtypeStruct((count, rank), sketch.dtype),
        ),
        in_specs=[pl.BlockSpec(memory_space=pltpu.VMEM)] * 2,
        out_specs=[pl.BlockSpec(memory_space=pltpu.VMEM)] * 3,
        scratch_shapes=[pltpu.VMEM((count, feats), points.dtype)]
        + [pltpu.SemaphoreType.DMA((copies,))] * 4,
        compiler_params=pltpu.CompilerParams(
            collective_id=0, has_side_effects=True, vmem_limit_bytes=24 * 1024 * 1024
        ),
    )(points.T, sketch)
    return pl.pallas_call(
        part_kernel,
        out_shape=(
            jax.ShapeDtypeStruct((own, rank), jnp.float32),
            jax.ShapeDtypeStruct((rank, rank), jnp.float32),
        ),
        in_specs=[pl.BlockSpec(memory_space=pltpu.VMEM)] * 3,
        out_specs=[pl.BlockSpec(memory_space=pltpu.VMEM)] * 2,
        scratch_shapes=[
            pltpu.VMEM((count, rank), jnp.bfloat16),
            pltpu.VMEM((count, rank), jnp.bfloat16),
            pltpu.VMEM((count, rank), jnp.float32),
            pltpu.VMEM((rank, rank), jnp.float32),
        ],
        compiler_params=pltpu.CompilerParams(vmem_limit_bytes=28 * 1024 * 1024),
    )(high, low, full)


def kernel_rows(block_t, cols_t, gamma):
    block_f = block_t.astype(jnp.float32)
    cols_f = cols_t.astype(jnp.float32)
    block_sq = jnp.sum(block_f * block_f, axis=0)
    cols_sq = jnp.sum(cols_f * cols_f, axis=0)
    cross = lax.dot_general(
        block_t, cols_t, (((0,), (0,)), ((), ())), preferred_element_type=jnp.float32
    )
    return jnp.exp(-gamma * (block_sq[:, None] + cols_sq[None, :] - 2.0 * cross))


def orthonormal(ymat, block_count):
    local_gram = jnp.dot(ymat.T, ymat, precision=lax.Precision.HIGHEST)
    gram = lax.psum(local_gram, ("col", "row")) / block_count
    lower = jnp.linalg.cholesky(gram)
    qmat = jax.scipy.linalg.solve_triangular(lower, ymat.T, lower=True).T
    return (qmat, lower.T)


def split_part(points, sketch):
    feats, own = points.shape
    block_count = own * lax.axis_size("col") * lax.axis_size("row")
    gamma = ((block_count / 32.0) ** (2.0 / feats) - 1.0) / 4.0
    row_pts = lax.all_gather(points, "row", axis=1, tiled=True)
    col_pts = lax.all_gather(points, "col", axis=1, tiled=True)

    def tile_at():
        return kernel_rows(row_pts, col_pts, gamma)

    def accumulate_fragment(piece):
        kernel_tile = tile_at()
        return jnp.dot(
            kernel_tile, piece, precision=lax.Precision.HIGHEST, preferred_element_type=jnp.float32
        )

    def apply_operator(vector_matrix):
        running_sum = accumulate_fragment(lax.all_gather(vector_matrix, "col", axis=0, tiled=True))
        return lax.psum_scatter(running_sum, "row", scatter_dimension=0, tiled=True)

    ymat = apply_operator(sketch)
    for step in range(PASSES):
        qmat, upper = orthonormal(ymat, block_count)
        ymat = apply_operator(qmat)
    basis, factor = orthonormal(ymat, block_count)
    return (basis, factor)


def local(points, sketch):
    count = points.shape[1] * lax.axis_size("col") * lax.axis_size("row")
    small = count <= MAX_POINTS and count % ROWS == 0
    pairs = lax.axis_size("col") % 2 == 0 and lax.axis_size("row") == 2
    if small and pairs and sketch.shape[1] == 2 * HALF and points.shape[1] % 16 == 0:
        return whole_part(points, sketch)
    return split_part(points, sketch)


def solution(mesh):
    in_specs = (P(None, ("groups", "col", "row")), P(("groups", "col", "row"), None))
    out_specs = (P(("groups", "col", "row"), None), P("groups", None))
    return jax.shard_map(local, mesh=mesh, in_specs=in_specs, out_specs=out_specs, check_vma=False)
```
